256 devices in a mesh: pair: 16 (over x, z_lo), tp: 8 (over y, z_hi), rep: 2 (over core).
Axes of the slice: x: 4, y: 4, z: 8 (z_hi: 2, z_lo: 4; z = z_hi * 4 + z_lo), core: 2. Of those that a mesh axis runs over, the one named last changes fastest.
Arguments:
- normed: bfloat16 [2, 16, 8192], P(None, 'rep', 'pair'), parts along dimension 1, may hold values from -6 to 6
- w_query: bfloat16 [8192, 8192], P('pair', 'tp'), may hold values from -0.0625 to 0.0625
- b_query: float32 [8192], P('tp'), may hold values from -3 to 3
- w_key: bfloat16 [8192, 1024], P('pair', 'tp'), may hold values from -0.25 to 0.25
- b_key: float32 [1024], P('tp'), may hold values from -8 to 8
- w_value: bfloat16 [8192, 1024], P('pair', 'tp'), may hold values from -0.0625 to 0.0625
- b_value: float32 [1024], P('tp'), may hold values from -5 to 5
- w_out: bfloat16 [8192, 8192], P('tp', 'pair'), may hold values from -0.5 to 0.5
- pool: bfloat16 [32, 8, 512, 16, 256], P(('rep', 'pair'), 'tp'), parts along dimension 0, as said below
- page_table: int32 [32, 512], P(('rep', 'pair')), parts along dimension 0, may hold values from 0 to 511, as said below
- lengths: int32 [16], P('rep'), parts along dimension 0, may hold values from 8192 to 12286, as said below
- plan: int32 [16, 2], P('rep'), parts along dimension 0, may hold values from 0 to 64, as said below
Outputs:
- attended: float32 [2, 16, 8192], P(None, 'rep', 'pair'), parts along dimension 1
- new_pool: bfloat16 [32, 8, 512, 16, 256], P(('rep', 'pair'), 'tp'), parts along dimension 0
The draws below stay inside these ranges and needn't reach their ends.
There are 2 independent parts, one for each index of `rep`. The reference program is written for one: setup_inputs(seed, part) draws one part's arguments, and reference() takes and returns one part's arrays. A program takes and returns all parts, laid end to end along the dimension named above; an argument that names none is the same for every part. Nothing has to cross between parts.
Inputs may be any that keep to these rules, and one draw needn't show every extreme that they name: `pool`: cached keys (first 128 entries of a slot row, already rotated) and values. `page_table`: each row is an order of the 512 slots of one pool. `lengths`: some request reaches the most. `plan`: some entry reaches the most.
All inputs are finite; a program needn't handle non-finite values.
Results may differ from the reference program's by a relative error of at most 0.011.
The reference program's roundings to bfloat16 on the way count: a program that leaves them out, or rounds other values in their place, can miss the bound.
Values may be sent and summed in bfloat16 or wider, within the bound.
A program may use at most 64 MiB of HBM per device.

```python
import math
import jax
import jax.numpy as jnp
from jax import lax

D = 8192
HD = 128
GROUP = 8
PAGE = 16
PAGES_HALF = 384
STEPS = 2
KV_HEADS = 8
Q_HEADS = 64
SECTION = 64
POOL_PAGES = 512
HALF = 6144
REQS = 8
N_PAIR = 16


def draw_pool(key, part):
    key = jax.random.fold_in(key, 11)
    key_part, value_part = jax.random.split(key, 2)
    half_shape = (N_PAIR, KV_HEADS, POOL_PAGES, PAGE, HD)
    key_rows = 1.5 * jax.random.normal(key_part, half_shape, jnp.float32)
    value_rows = jax.random.normal(value_part, half_shape, jnp.float32)
    return jnp.concatenate([key_rows, value_rows], -1).astype(jnp.bfloat16)


def draw_page_table(key, part):
    key = jax.random.fold_in(key, 12)
    row_keys = jax.random.split(key, N_PAIR)
    orders = jax.vmap(lambda row_key: jax.random.permutation(row_key, POOL_PAGES))(row_keys)
    return orders.astype(jnp.int32)


def draw_lengths(key, part):
    key = jax.random.fold_in(key, 13)
    spread_part, pick_part = jax.random.split(key, 2)
    lowest = HALF + PAGE * STEPS * SECTION
    span = HALF - PAGE * STEPS * SECTION - STEPS
    drawn = lowest + jax.random.randint(spread_part, (REQS,), 0, span + 1)
    chosen = jax.random.randint(pick_part, (), 0, REQS)
    return jnp.where(jnp.arange(REQS) == chosen, lowest + span, drawn).astype(jnp.int32)


def draw_plan(key, part):
    key = jax.random.fold_in(key, 14)
    count_part, pick_part = jax.random.split(key, 2)
    drawn = jax.random.randint(count_part, (REQS * STEPS,), 0, SECTION + 1)
    chosen = jax.random.randint(pick_part, (), 0, REQS * STEPS)
    filled = jnp.where(jnp.arange(REQS * STEPS) == chosen, SECTION, drawn)
    return filled.reshape(REQS, STEPS).astype(jnp.int32)


def block_scale(key, shape, cuts, low, largest):
    loudness, own = 1.0, jax.random.fold_in(key, 6)
    for axis_at, blocks in cuts:
        steps = jnp.exp(jax.random.uniform(jax.random.fold_in(own, axis_at), (blocks,), jnp.float32, low / len(cuts), largest / len(cuts)))
        loudness = loudness * jnp.repeat(steps, shape[axis_at] // blocks).reshape([-1 if axis == axis_at else 1 for axis in range(len(shape))])
    return loudness


def normal_values(stream_key, dims, spread, most, cuts=(), kind=jnp.bfloat16):
    gain = block_scale(stream_key, dims, cuts, -0.22, 0.18) if cuts else 1.0
    array = jax.random.normal(stream_key, dims, jnp.float32) * spread * gain
    return jnp.minimum(jnp.maximum(array, -most), most).astype(kind)


def setup_inputs(seed: int = 0, part: int = 0) -> dict:
    arg_keys = jax.random.split(jax.random.key(seed), 13)
    part_keys = jax.random.split(jax.random.fold_in(arg_keys[12], part), 13)
    normed = normal_values(part_keys[0], (STEPS, REQS, D), 1.0, 6.0, ((2, 16),))
    w_query = normal_values(arg_keys[1], (D, Q_HEADS * HD), D ** -0.5, 0.0625, ((0, 16), (1, 8)))
    b_query = normal_values(arg_keys[2], (Q_HEADS * HD,), 0.5, 3.0, ((0, 8),), jnp.float32)
    w_key = normal_values(arg_keys[3], (D, KV_HEADS * HD), (D // 16) ** -0.5, 0.25, ((0, 16), (1, 8)))
    b_key = normal_values(arg_keys[4], (KV_HEADS * HD,), 2.0, 8.0, ((0, 8),), jnp.float32)
    w_value = normal_values(arg_keys[5], (D, KV_HEADS * HD), D ** -0.5, 0.0625, ((0, 16), (1, 8)))
    b_value = normal_values(arg_keys[6], (KV_HEADS * HD,), 1.0, 5.0, ((0, 8),), jnp.float32)
    w_out = normal_values(arg_keys[7], (Q_HEADS * HD, D), HD ** -0.5, 0.5, ((0, 8), (1, 16)))
    pool = draw_pool(jax.random.fold_in(jax.random.fold_in(arg_keys[12], part), 71), part)
    page_table = draw_page_table(jax.random.fold_in(jax.random.fold_in(arg_keys[12], part), 71), part)
    lengths = draw_lengths(jax.random.fold_in(jax.random.fold_in(arg_keys[12], part), 71), part)
    plan = draw_plan(jax.random.fold_in(jax.random.fold_in(arg_keys[12], part), 71), part)
    return dict(normed=normed, w_query=w_query, b_query=b_query, w_key=w_key, b_key=b_key, w_value=w_value, b_value=b_value, w_out=w_out, pool=pool, page_table=page_table, lengths=lengths, plan=plan)


rope_base = 1000000.0

def rotate(vectors, position):
    half_size = vectors.shape[-1] // 2
    frequency = rope_base ** (-(jnp.arange(half_size, dtype=jnp.float32) * 2.0 / vectors.shape[-1]))
    angles = position * frequency
    cosine = jnp.cos(angles)
    sine_val = jnp.sin(angles)
    first_half = vectors[..., :half_size]
    second_half = vectors[..., half_size:]
    return jnp.concatenate([first_half * cosine - second_half * sine_val, second_half * cosine + first_half * sine_val], -1)

def reference(normed, w_query, b_query, w_key, b_key, w_value, b_value, w_out, pool, page_table, lengths, plan):
    score_scale = 1.0 / math.sqrt(HD)
    target_pools = [pool[request] for request in range(REQS)]
    source_pools = [pool[REQS + request] for request in range(REQS)]
    section_ids = jnp.arange(SECTION, dtype=jnp.int32)
    anchor = jnp.int32(0)
    results = []
    for step_index in range(STEPS):
        hidden = normed[step_index]
        query = jnp.dot(hidden, w_query, preferred_element_type=jnp.float32) + b_query
        key_new = jnp.dot(hidden, w_key, preferred_element_type=jnp.float32) + b_key
        value_new = jnp.dot(hidden, w_value, preferred_element_type=jnp.float32) + b_value
        position = (lengths + step_index).astype(jnp.float32)[:, None, None]
        query_rot = rotate(query.reshape(REQS, Q_HEADS, HD), position).astype(jnp.bfloat16)
        key_rot = rotate(key_new.reshape(REQS, KV_HEADS, HD), position).astype(jnp.bfloat16)
        value_rot = value_new.reshape(REQS, KV_HEADS, HD).astype(jnp.bfloat16)
        head_list = []
        for request in range(REQS):
            offset = (lengths[request] - HALF + step_index).astype(jnp.int32)
            write_slot = page_table[REQS + request, offset // PAGE].astype(jnp.int32)
            new_entry = jnp.concatenate([key_rot[request], value_rot[request]], -1)[:, None, None, :]
            source_pools[request] = lax.dynamic_update_slice(source_pools[request], new_entry, (anchor, write_slot, (offset % PAGE).astype(jnp.int32), anchor))
            before = jnp.sum(plan[request, :step_index]).astype(jnp.int32)
            page_picks = before + section_ids
            from_slots = page_table[REQS + request][page_picks]
            to_slots = page_table[request][PAGES_HALF + page_picks]
            keep_mask = section_ids < plan[request, step_index]
            moved = jnp.where(keep_mask[None, :, None, None], source_pools[request][:, from_slots], target_pools[request][:, to_slots])
            target_pools[request] = target_pools[request].at[:, to_slots].set(moved)
            own_pages = target_pools[request][:, page_table[request, :PAGES_HALF]]
            far_pages = source_pools[request][:, page_table[REQS + request, :PAGES_HALF]]
            context = jnp.concatenate([own_pages, far_pages], 1).reshape(KV_HEADS, 2 * HALF, 2 * HD)
            token_ids = jnp.arange(2 * HALF, dtype=jnp.int32)
            visible = token_ids <= lengths[request] + step_index
            key_rows = context[:, :, :HD].astype(jnp.float32)
            value_rows = context[:, :, HD:].astype(jnp.float32)
            head_query = query_rot[request].reshape(KV_HEADS, GROUP, HD).astype(jnp.float32)
            scores = jnp.einsum('hgd,htd->hgt', head_query, key_rows) * score_scale
            scores = jnp.where(visible[None, None, :], scores, -1e+30)
            row_max = lax.optimization_barrier(jnp.max(scores, -1, keepdims=True))
            weights = jnp.where(visible[None, None, :], jnp.exp(scores - row_max), 0.0)
            row_sum = lax.optimization_barrier(jnp.sum(weights, -1, keepdims=True))
            rounded = weights.astype(jnp.bfloat16).astype(jnp.float32)
            head_out = jnp.einsum('hgt,htd->hgd', rounded, value_rows) / row_sum
            head_list.append(head_out.reshape(Q_HEADS * HD))
        attended_rows = jnp.stack(head_list).astype(jnp.bfloat16)
        results.append(jnp.dot(attended_rows, w_out, preferred_element_type=jnp.float32))
    new_pool = jnp.stack(target_pools + source_pools)
    return (jnp.stack(results), new_pool)
```

```python
import functools
import math

import jax
import jax.numpy as jnp
import numpy as np
from jax import lax
from jax.experimental import pallas as pl
from jax.experimental.pallas import tpu as pltpu
from jax.sharding import PartitionSpec as P

MESH = pl.DeviceIdType.MESH
PAGES_HALF = 384
SECTION = 64
STEPS = 2
BASE = 1000000.0
LANES = 128
RING = 4
NEW_ROWS = 8
CHUNK = 64


def sin_cos(angle):
    turns = jnp.floor(angle * (2.0 / math.pi) + 0.5)
    rest = angle - turns * 1.5703125
    rest = rest - turns * 4.837512969970703125e-4
    rest = rest - turns * 7.54978995489188216e-8
    sq = rest * rest
    sine = rest + rest * sq * (
        -1.6666654611e-1 + sq * (8.3321608736e-3 + sq * -1.9515295891e-4)
    )
    cosine = (
        1.0
        - 0.5 * sq
        + sq * sq * (4.166664568298827e-2 + sq * (-1.388731625493765e-3 + sq * 2.443315711809948e-5))
    )
    quarter = turns - 4.0 * jnp.floor(turns * 0.25)
    swap = (quarter == 1.0) | (quarter == 3.0)
    sine_out = jnp.where(swap, cosine, sine)
    cosine_out = jnp.where(swap, sine, cosine)
    sine_out = jnp.where(quarter >= 2.0, -sine_out, sine_out)
    cosine_out = jnp.where((quarter == 1.0) | (quarter == 2.0), -cosine_out, cosine_out)
    return sine_out, cosine_out


def attend_kernel(
    pair_count,
    tp_count,
    normed,
    w_query,
    b_query,
    w_key,
    b_key,
    w_value,
    b_value,
    w_out,
    pool,
    table,
    lengths,
    freq,
    attended,
    incoming,
    fresh,
    pages,
    hidden_v,
    bias_q,
    bias_k,
    bias_v,
    table_s,
    table_v,
    length_s,
    freq_v,
    wq,
    wk,
    wv,
    wo,
    outgoing,
    passing,
    part,
    parts,
    scores,
    bias,
    half,
    halves,
    merged,
    proj,
    projs,
    load_sem,
    s1,
    r1,
    s1_new,
    r1_new,
    s2,
    r2,
    s3,
    r3,
    sm,
    rm,
    rp,
    sf,
    ready,
):
    requests = pair_count // 2
    me = lax.axis_index("pair")
    tp = lax.axis_index("tp")
    request = lax.rem(me, requests)
    source = me >= requests
    pair_peers = [lax.rem(me + d, pair_count) for d in range(1, pair_count)]
    tp_peers = [lax.rem(tp + d, tp_count) for d in range(1, tp_count)]

    far = lax.rem(tp, 2)
    near_peers = [lax.rem(tp + d, tp_count) for d in range(2, tp_count, 2)]
    far_peers = [lax.rem(tp + d, tp_count) for d in range(1, tp_count, 2)]
    barrier = pltpu.get_barrier_semaphore()
    for q in pair_peers:
        pl.semaphore_signal(barrier, inc=1, device_id={"pair": q}, device_id_type=MESH)
    for q in near_peers:
        pl.semaphore_signal(barrier, inc=1, device_id={"tp": q}, device_id_type=MESH)

    @pl.when(far == 0)
    def _():
        for q in far_peers:
            pl.semaphore_signal(barrier, inc=1, device_id={"tp": q}, device_id_type=MESH)

    operands = (
        (normed, hidden_v),
        (w_query, wq),
        (w_key, wk),
        (w_value, wv),
        (table, table_s),
        (pool.at[0, 0], pages),
        (table, table_v),
        (lengths, length_s),
        (freq, freq_v),
        (b_query, bias_q),
        (b_key, bias_k),
        (b_value, bias_v),
        (w_out, wo),
    )
    loads = [
        pltpu.make_async_copy(here, there, load_sem.at[i])
        for i, (here, there) in enumerate(operands)
    ]
    for load in loads:
        load.start()

    part[...] = jnp.zeros(part.shape, part.dtype)
    heads = wq.shape[1] // LANES
    loads[0].wait()
    hidden = hidden_v[...].reshape(STEPS * requests, hidden_v.shape[2])
    loads[1].wait()
    query = jnp.dot(hidden, wq[...], preferred_element_type=jnp.float32)
    for s in range(STEPS):
        for h in range(heads):
            part[:, s * heads + h, :] = query[
                s * requests : (s + 1) * requests, h * LANES : (h + 1) * LANES
            ]
    loads[2].wait()
    loads[3].wait()
    key = jnp.dot(hidden, wk[...], preferred_element_type=jnp.float32)
    value = jnp.dot(hidden, wv[...], preferred_element_type=jnp.float32)
    count = STEPS * heads
    for s in range(STEPS):
        part[:, count + s, :] = key[s * requests : (s + 1) * requests]
        part[:, count + STEPS + s, :] = value[s * requests : (s + 1) * requests]

    loads[4].wait()
    loads[5].wait()

    @pl.when(source)
    def _():
        for i in range(STEPS * SECTION):
            outgoing[i] = pages[table_s[0, i]]

    pl.semaphore_wait(barrier, pair_count - 1 + len(near_peers) + far * len(far_peers))

    @pl.when(far == 1)
    def _():
        for q in far_peers:
            pl.semaphore_signal(ready, inc=1, device_id={"tp": q}, device_id_type=MESH)

    first = []
    first_new = []
    for d in range(1, pair_count):
        peer = pair_peers[d - 1]
        at = lax.rem(peer, requests)
        copy = pltpu.make_async_remote_copy(
            src_ref=part.at[at, pl.ds(0, count)],
            dst_ref=parts.at[me, pl.ds(0, count)],
            send_sem=s1.at[d - 1],
            recv_sem=r1.at[d - 1],
            device_id={"pair": peer},
            device_id_type=MESH,
        )
        copy.start()
        first.append(copy)
        copy = pltpu.make_async_remote_copy(
            src_ref=part.at[at, pl.ds(count, NEW_ROWS)],
            dst_ref=parts.at[me, pl.ds(count, NEW_ROWS)],
            send_sem=s1_new.at[d - 1],
            recv_sem=r1_new.at[d - 1],
            device_id={"pair": peer},
            device_id_type=MESH,
        )

        @pl.when(peer >= requests)
        def _():
            copy.start()

        first_new.append(copy)

    column = pair_count // RING
    up, down = lax.rem(me + column, pair_count), lax.rem(me + pair_count - column, pair_count)
    section = outgoing.shape[0] // 2
    moves = [
        pltpu.make_async_remote_copy(
            src_ref=outgoing.at[pl.ds(i * section, section)],
            dst_ref=passing,
            send_sem=sm.at[i],
            recv_sem=rp,
            device_id={"pair": way},
            device_id_type=MESH,
        )
        for i, way in enumerate((up, down))
    ]

    @pl.when(source)
    def _():
        for move in moves:
            move.start()

    parts[me] = part[request]

    for load in loads[6:12]:
        load.wait()
    length = length_s[request]
    half_tokens = PAGES_HALF * pages.shape[1]
    limit = jnp.where(source, length - half_tokens, half_tokens)
    slots = pages.shape[0]
    page_len = pages.shape[1]
    per_row = LANES // page_len
    order = table_v[...]
    start = lax.broadcasted_iota(jnp.int32, (1, slots), 1) * page_len
    kept = jnp.clip(limit - start, 0, page_len).astype(jnp.float32)
    row_of = lax.broadcasted_iota(jnp.int32, (slots // per_row, slots), 0)
    lane_of = lax.broadcasted_iota(jnp.int32, (LANES, slots), 0)
    hit_row = jnp.where((order // per_row) == row_of, 1.0, 0.0).astype(jnp.bfloat16)
    hit_lane = jnp.where((order % per_row) == (lane_of // page_len), kept, 0.0).astype(jnp.bfloat16)
    seen = lax.dot_general(
        hit_row, hit_lane, (((1,), (1,)), ((), ())), preferred_element_type=jnp.float32
    )
    lane = lax.broadcasted_iota(jnp.int32, seen.shape, 1)
    bias[...] = jnp.where((lane % page_len).astype(jnp.float32) < seen, 0.0, -1e30)

    row = lax.broadcasted_iota(jnp.int32, (count + NEW_ROWS, LANES), 0)
    step = jnp.where(row < count, row // heads, row - count)
    angle = (length + step).astype(jnp.float32) * freq_v[...]
    sine, cosine = sin_cos(angle)
    lane = lax.broadcasted_iota(jnp.int32, (count + NEW_ROWS, LANES), 1)
    sine = jnp.where(lane < LANES // 2, -sine, sine)
    turned = row < count + STEPS
    query_bias = bias_q[...].reshape(heads, LANES)
    key_bias = bias_k[...].reshape(1, LANES)
    value_bias = bias_v[...].reshape(1, LANES)
    rest = row[count:]
    add = jnp.concatenate(
        [query_bias] * STEPS
        + [
            jnp.where(
                rest < count + STEPS,
                key_bias,
                jnp.where(rest < count + 2 * STEPS, value_bias, 0.0),
            )
        ],
        0,
    )

    for d in range(1, pair_count):
        first[d - 1].wait()

        @pl.when(pair_peers[d - 1] >= requests)
        def _():
            first_new[d - 1].wait_send()

    @pl.when(source)
    def _():
        for copy in first_new:
            copy.wait_recv()

    total = add
    for p in range(pair_count):
        total = total + parts[p]
    rotated = total * cosine + pltpu.roll(total, LANES // 2, 1) * sine
    total = jnp.where(turned, rotated, total)
    queries = total[:count].astype(jnp.bfloat16)
    new = jnp.where(source, total[count:], 0.0)
    fresh[...] = new
    new_rows = new.astype(jnp.bfloat16)
    new_values = pltpu.roll(new, NEW_ROWS - STEPS, 0).astype(jnp.bfloat16)

    scale = 1.0 / math.sqrt(LANES)
    contract_last = (((1,), (1,)), ((), ()))
    own = lax.dot_general(queries, new_rows, contract_last, preferred_element_type=jnp.float32)
    own = own * scale
    token = lax.broadcasted_iota(jnp.int32, own.shape, 1)
    own_step = lax.broadcasted_iota(jnp.int32, own.shape, 0) // heads
    own_seen = (token <= own_step) & (token < jnp.where(source, STEPS, 0))
    own = jnp.where(own_seen, own, -1e30)

    chunk_tokens = CHUNK * page_len
    chunks = slots // CHUNK
    tiles = chunk_tokens // LANES
    highest = jnp.full((count, LANES), -1e30, jnp.float32)
    for c in range(chunks):
        keys = pages[pl.ds(c * CHUNK, CHUNK), :, pl.ds(0, LANES)].reshape(chunk_tokens, LANES)
        score = lax.dot_general(queries, keys, contract_last, preferred_element_type=jnp.float32)
        for t in range(tiles):
            tile = score[:, t * LANES : (t + 1) * LANES] * scale + bias[pl.ds(c * tiles + t, 1), :]
            scores[c * tiles + t] = tile
            highest = jnp.maximum(highest, tile)
    top = jnp.maximum(jnp.max(highest, 1, keepdims=True), jnp.max(own, 1, keepdims=True))
    own_weight = jnp.where(own_seen, jnp.exp(own - top), 0.0)
    sums = jnp.zeros((count, LANES), jnp.float32)
    out = jnp.dot(
        own_weight.astype(jnp.bfloat16), new_values, preferred_element_type=jnp.float32
    )
    for c in range(chunks):
        weights = []
        for t in range(tiles):
            weight = jnp.exp(scores[c * tiles + t] - top)
            sums = sums + weight
            weights.append(weight.astype(jnp.bfloat16))
        values = pages[pl.ds(c * CHUNK, CHUNK), :, pl.ds(LANES, LANES)].reshape(chunk_tokens, LANES)
        out = out + jnp.dot(
            jnp.concatenate(weights, 1), values, preferred_element_type=jnp.float32
        )
    mass = jnp.sum(sums, 1, keepdims=True) + jnp.sum(own_weight, 1, keepdims=True)

    half[pl.ds(0, count), :] = (out / mass).astype(jnp.bfloat16)
    lane = lax.broadcasted_iota(jnp.int32, (count, LANES), 1)
    stats = jnp.where(lane < 3, top, jnp.where(lane < 6, mass, 0.0))
    high = stats.astype(jnp.bfloat16).astype(jnp.float32)
    middle = (stats - high).astype(jnp.bfloat16).astype(jnp.float32)
    low = stats - high - middle
    addend = lane % 3
    stats = jnp.where(addend == 0, high, jnp.where(addend == 1, middle, low))
    half[pl.ds(count, count), :] = stats.astype(jnp.bfloat16)

    second = []
    for d in range(1, pair_count):
        copy = pltpu.make_async_remote_copy(
            src_ref=half,
            dst_ref=halves.at[me],
            send_sem=s2.at[d - 1],
            recv_sem=r2.at[d - 1],
            device_id={"pair": pair_peers[d - 1]},
            device_id_type=MESH,
        )
        copy.start()
        second.append(copy)

    upward = (me < column) | (me >= pair_count - column)
    forward = pltpu.make_async_remote_copy(
        src_ref=passing,
        dst_ref=incoming.at[pl.ds(jnp.where(upward, 0, section), section)],
        send_sem=sf,
        recv_sem=rm.at[jnp.where(upward, 0, 1)],
        device_id={"pair": jnp.where(upward, up, down)},
        device_id_type=MESH,
    )
    moves[0].wait_recv()
    forward.start()

    halves[me] = half[...]
    loads[12].wait()
    pick_row = lax.broadcasted_iota(jnp.int32, (LANES, 2 * LANES), 0)
    pick_lane = lax.broadcasted_iota(jnp.int32, (LANES, 2 * LANES), 1)
    pick = (pick_row < 6) & ((pick_row // 3) == (pick_lane // LANES))
    pick = jnp.where(pick, 1.0, 0.0).astype(jnp.bfloat16)
    for copy in second:
        copy.wait()

    many = requests * count

    def side(at):
        block = halves[pl.ds(at, requests)]
        result = block[:, :count].reshape(many, LANES).astype(jnp.float32)
        stat = jnp.dot(
            block[:, count:].reshape(many, LANES), pick, preferred_element_type=jnp.float32
        )
        return result, stat[:, :LANES], stat[:, LANES:]

    out_a, top_a, mass_a = side(0)
    out_b, top_b, mass_b = side(requests)
    joint = jnp.maximum(top_a, top_b)
    weight_a = mass_a * jnp.exp(top_a - joint)
    weight_b = mass_b * jnp.exp(top_b - joint)
    head_out = (weight_a * out_a + weight_b * out_b) / (weight_a + weight_b)
    merged[...] = head_out.reshape(requests, count, LANES)
    blocks = []
    for h in range(heads):
        blocks.append(
            jnp.concatenate([merged[:, s * heads + h, :] for s in range(STEPS)], 0)
        )
    attended_rows = jnp.concatenate(blocks, 1).astype(jnp.bfloat16)
    proj[...] = jnp.dot(
        attended_rows, wo[...], preferred_element_type=jnp.float32
    ).astype(jnp.bfloat16)

    @pl.when(far == 0)
    def _():
        pl.semaphore_wait(ready, len(far_peers))

    third = []
    for d in range(1, tp_count):
        copy = pltpu.make_async_remote_copy(
            src_ref=proj,
            dst_ref=projs.at[tp],
            send_sem=s3.at[d - 1],
            recv_sem=r3.at[d - 1],
            device_id={"tp": tp_peers[d - 1]},
            device_id_type=MESH,
        )
        copy.start()
        third.append(copy)
    projs[tp] = proj[...]
    for copy in third:
        copy.wait()
    result = projs[0].astype(jnp.float32)
    for t in range(1, tp_count):
        result = result + projs[t].astype(jnp.float32)
    attended[...] = result.reshape(attended.shape)

    @pl.when(source)
    def _():
        for move in moves:
            move.wait_send()

    forward.wait_send()

    @pl.when(jnp.logical_not(source))
    def _():
        for i in range(2):
            pltpu.make_async_remote_copy(
                src_ref=passing,
                dst_ref=incoming.at[pl.ds(i * section, section)],
                send_sem=sf,
                recv_sem=rm.at[i],
                device_id={"pair": up},
                device_id_type=MESH,
            ).wait_recv()


def pool_kernel(
    requests,
    base,
    incoming,
    fresh,
    result,
    table,
    lengths,
    plan,
    attended,
    new_pool,
    pages,
    table_s,
    length_s,
    plan_s,
    load_sem,
    store_sem,
):
    del base
    me = lax.axis_index("pair")
    request = lax.rem(me, requests)
    source = me >= requests
    page_len = pages.shape[1]
    operands = ((table, table_s), (lengths, length_s), (plan, plan_s))
    loads = [
        pltpu.make_async_copy(here, there, load_sem.at[i])
        for i, (here, there) in enumerate(operands)
    ]
    for load in loads:
        load.start()
    store_result = pltpu.make_async_copy(result, attended, store_sem.at[0])
    store_result.start()
    for load in loads:
        load.wait()

    @pl.when(jnp.logical_not(source))
    def _():
        handed = plan_s[0, request] + plan_s[1, request]

        def put(i, carry):
            pages[table_s[0, PAGES_HALF + i]] = incoming[i]
            return carry

        lax.fori_loop(0, handed, put, 0)

    @pl.when(source)
    def _():
        for s in range(STEPS):
            offset = length_s[request] - PAGES_HALF * page_len + s
            slot = table_s[0, offset // page_len]
            line = offset % page_len
            entry = jnp.concatenate([fresh[pl.ds(s, 1), :], fresh[pl.ds(STEPS + s, 1), :]], 1)
            old = pages[slot].astype(jnp.float32)
            at = lax.broadcasted_iota(jnp.int32, old.shape, 0)
            pages[slot] = jnp.where(at == line, entry, old).astype(pages.dtype)

    store = pltpu.make_async_copy(pages, new_pool.at[0, 0], store_sem.at[1])
    store.start()
    store_result.wait()
    store.wait()


def local(
    normed, w_query, b_query, w_key, b_key, w_value, b_value, w_out, pool, page_table, lengths, plan
):
    pair_count = lax.axis_size("pair")
    tp_count = lax.axis_size("tp")
    requests = pair_count // 2
    head_size = w_key.shape[1]
    heads = w_query.shape[1] // head_size
    count = STEPS * heads
    slots, page_len, width = pool.shape[2:]
    moved = STEPS * SECTION
    model = w_query.shape[0]
    out_width = w_out.shape[1]
    half_index = np.arange(head_size) % (head_size // 2)
    freq = jnp.asarray(
        (BASE ** (-(half_index * 2.0 / head_size))).astype(np.float32)[None, :]
    )
    bf16, f32 = jnp.bfloat16, jnp.float32
    vmem = pl.BlockSpec(memory_space=pltpu.VMEM)
    hbm = pl.BlockSpec(memory_space=pltpu.HBM)
    dma = pltpu.SemaphoreType.DMA
    regular = pltpu.SemaphoreType.REGULAR
    others = pair_count - 1
    keep = functools.partial(pltpu.with_memory_space_constraint, memory_space=pltpu.HBM)
    near = functools.partial(pltpu.with_memory_space_constraint, memory_space=pltpu.VMEM)
    operands = (
        normed, w_query, b_query, w_key, b_key, w_value, b_value, w_out, pool,
        page_table, lengths, freq,
    )
    attended, incoming, fresh, pages = pl.pallas_call(
        functools.partial(attend_kernel, pair_count, tp_count),
        name="attend",
        out_shape=(
            pltpu.VMEM(normed.shape[:2] + (out_width,), f32),
            pltpu.VMEM((moved, page_len, width), bf16),
            pltpu.VMEM((NEW_ROWS, head_size), f32),
            pltpu.VMEM((slots, page_len, width), bf16),
        ),
        in_specs=[hbm] * len(operands),
        out_specs=(vmem,) * 4,
        scratch_shapes=[
            pltpu.VMEM(normed.shape, bf16),
            pltpu.VMEM(b_query.shape, f32),
            pltpu.VMEM(b_key.shape, f32),
            pltpu.VMEM(b_value.shape, f32),
            pltpu.SMEM(page_table.shape, jnp.int32),
            pltpu.VMEM(page_table.shape, jnp.int32),
            pltpu.SMEM(lengths.shape, jnp.int32),
            pltpu.VMEM(freq.shape, f32),
            pltpu.VMEM((model, heads * head_size), bf16),
            pltpu.VMEM((model, head_size), bf16),
            pltpu.VMEM((model, head_size), bf16),
            pltpu.VMEM((heads * head_size, out_width), bf16),
            pltpu.VMEM((moved, page_len, width), bf16),
            pltpu.VMEM((moved // 2, page_len, width), bf16),
            pltpu.VMEM((requests, count + NEW_ROWS, head_size), f32),
            pltpu.VMEM((pair_count, count + NEW_ROWS, head_size), f32),
            pltpu.VMEM((slots * page_len // LANES, count, LANES), f32),
            pltpu.VMEM((slots * page_len // LANES, LANES), f32),
            pltpu.VMEM((2 * count, head_size), bf16),
            pltpu.VMEM((pair_count, 2 * count, head_size), bf16),
            pltpu.VMEM((requests, count, head_size), f32),
            pltpu.VMEM((STEPS * requests, out_width), bf16),
            pltpu.VMEM((tp_count, STEPS * requests, out_width), bf16),
            dma((13,)),
            dma((others,)),
            dma((others,)),
            dma((others,)),
            dma((others,)),
            dma((others,)),
            dma((others,)),
            dma((tp_count - 1,)),
            dma((tp_count - 1,)),
            dma((2,)),
            dma((2,)),
            dma,
            dma,
            regular,
        ],
        compiler_params=pltpu.CompilerParams(
            collective_id=0, has_side_effects=True, vmem_limit_bytes=28 * 2**20
        ),
    )(*(keep(x) for x in operands))
    attended, new_pool, _ = pl.pallas_call(
        functools.partial(pool_kernel, requests),
        name="place",
        out_shape=(
            pltpu.HBM(attended.shape, f32),
            pltpu.HBM(pool.shape, bf16),
            pltpu.VMEM(pages.shape, bf16),
        ),
        in_specs=[vmem] * 7,
        out_specs=(hbm, hbm, vmem),
        input_output_aliases={0: 2},
        scratch_shapes=[
            pltpu.SMEM(page_table.shape, jnp.int32),
            pltpu.SMEM(lengths.shape, jnp.int32),
            pltpu.SMEM(plan.shape[::-1], jnp.int32),
            dma((3,)),
            dma((2,)),
        ],
        compiler_params=pltpu.CompilerParams(vmem_limit_bytes=8 * 2**20),
    )(*(near(x) for x in (pages, incoming, fresh, attended, page_table, lengths, plan.T)))
    return attended, new_pool


def solution(mesh):
    return jax.shard_map(
        local,
        mesh=mesh,
        in_specs=(
            P(None, "rep", "pair"),
            P("pair", "tp"),
            P("tp"),
            P("pair", "tp"),
            P("tp"),
            P("pair", "tp"),
            P("tp"),
            P("tp", "pair"),
            P(("rep", "pair"), "tp", None, None, None),
            P(("rep", "pair"), None),
            P("rep"),
            P("rep", None),
        ),
        out_specs=(P(None, "rep", "pair"), P(("rep", "pair"), "tp", None, None, None)),
        check_vma=False,
    )
```
